32 devices in a mesh: groups: 2 (over y), inner: 4 (over z), outer: 2 (over x), heads: 2 (over core).
Axes of the slice: x: 2, y: 2, z: 4, core: 2. Of those that a mesh axis runs over, the one named last changes fastest.
Arguments:
- queries: bfloat16 [2048, 64, 128], P(('groups', 'inner'), ('outer', 'heads')), parts along dimension 0, may hold values from -6 to 6
- keys: bfloat16 [2048, 8, 128], P(('groups', 'inner')), parts along dimension 0, may hold values from -6 to 6
- values: bfloat16 [2048, 8, 128], P(('groups', 'inner')), parts along dimension 0, may hold values from -6 to 6
- grad_out: bfloat16 [2048, 64, 128], P(('groups', 'inner'), ('outer', 'heads')), parts along dimension 0, may hold values from -6 to 6
- seg_ids: int32 [2048], P(('groups', 'inner')), parts along dimension 0, may hold values from 0 to 3, never falling along the last dimension, each value on 1 to 512 neighbouring positions
Outputs:
- attn_out: bfloat16 [2048, 64, 128], P(('groups', 'inner'), ('outer', 'heads')), parts along dimension 0
- grad_q: bfloat16 [2048, 64, 128], P(('groups', 'inner'), ('outer', 'heads')), parts along dimension 0
- grad_k: bfloat16 [2048, 8, 128], P(('groups', 'inner')), parts along dimension 0
- grad_v: bfloat16 [2048, 8, 128], P(('groups', 'inner')), parts along dimension 0
The draws below stay inside these ranges and needn't reach their ends.
There are 2 independent parts, one for each index of `groups`. The reference program is written for one: setup_inputs(seed, part) draws one part's arguments, and reference() takes and returns one part's arrays. A program takes and returns all parts, laid end to end along the dimension named above; each array names one. Nothing has to cross between parts.
Inputs may be any that keep to these rules, and one draw needn't show every extreme that they name: `seg_ids`: trajectory numbers never fall along the sequence; each trajectory holds 1 to 512 consecutive tokens, and one holds exactly 512.
All inputs are finite; a program needn't handle non-finite values.
Results may differ from the reference program's by a relative error of at most 0.0073.
Values may be sent and summed in bfloat16 or wider, within the bound.
A program may use at most 64 MiB of HBM per device.

```python
import math
import jax
import jax.numpy as jnp
import numpy as np
from jax import lax

HEAD_DIM = 128
GROUP = 8
KV_HEADS = 8
TOK_DEV = 256
SPAN = 2
HEADS = 64
LENGTH = 1024
SEG_MOST = 512
SEGS = 4


def draw_queries(key, part):
    key = jax.random.fold_in(key, 11)
    entries = jnp.clip(jax.random.normal(key, (LENGTH, HEADS, HEAD_DIM), jnp.float32), -6.0, 6.0)
    return entries.astype(jnp.bfloat16)


def draw_keys(key, part):
    key = jax.random.fold_in(key, 12)
    entries = jnp.clip(jax.random.normal(key, (LENGTH, KV_HEADS, HEAD_DIM), jnp.float32), -6.0, 6.0)
    return entries.astype(jnp.bfloat16)


def level_of(stream_key, dims, pieces, smallest, largest):
    def one(axis_at, parts):
        draws = jax.random.uniform(jax.random.fold_in(jax.random.fold_in(stream_key, 6), axis_at), (parts,), jnp.float32, smallest / len(pieces), largest / len(pieces))
        return jnp.repeat(jnp.exp(draws), dims[axis_at] // parts).reshape((-1,) + (1,) * (len(dims) - axis_at - 1))

    gain = one(*pieces[0])
    for cut in pieces[1:]:
        gain = gain * one(*cut)
    return gain


def split_up(count, total, reach, lean):
    loads = [(1 << 20) // math.isqrt(rank ** lean) + 1 for rank in range(2, count + 1)]
    rest, given = total - reach - (count - 1), [1] * (count - 1)
    while rest > 0:
        free = [i for i in range(count - 1) if given[i] < reach]
        pool, left = sum([loads[i] for i in free]), rest
        for i in free:
            more = min(reach - given[i], max(1, left * loads[i] // pool), rest)
            given[i] = given[i] + more
            rest = rest - more
    return np.array([reach] + given)


def ragged_sizes(own_key, count, total, limit, skew):
    if count == 2:
        one = jax.random.randint(own_key, (), max(1, total - limit), min(limit, total - 1) + 1)
        return jnp.stack([one, total - one])
    sizes = jnp.asarray(split_up(count, total, limit, skew), jnp.int32)
    twos = (count - 1) // 2
    source_of, receiver = sizes[1:1 + 2 * twos:2], sizes[2:2 + 2 * twos:2]
    margin = jnp.minimum(source_of - 1, limit - receiver)
    shifted = jax.random.randint(jax.random.fold_in(own_key, 1), (twos,), 0, 1 << 20) % (margin + 1)
    sizes = sizes.at[1:1 + 2 * twos:2].set(source_of - shifted).at[2:2 + 2 * twos:2].set(receiver + shifted)
    return sizes[jax.random.permutation(jax.random.fold_in(own_key, 2), count)]


def scatter_about(own_key, extent, scale, limit, cuts=(), held_as=jnp.bfloat16):
    values = scale * jax.random.normal(own_key, extent, jnp.float32)
    if cuts:
        values = values * level_of(own_key, extent, cuts, -0.22, 0.18)
    return jnp.clip(values, -limit, limit).astype(held_as)


def setup_inputs(seed: int = 0, part: int = 0) -> dict:
    streams_of = jax.random.split(jax.random.key(seed), 6)
    part_splits = jax.random.split(jax.random.fold_in(streams_of[5], part), 6)
    return {
        "queries": draw_queries(jax.random.fold_in(jax.random.fold_in(streams_of[5], part), 71), part),
        "keys": draw_keys(jax.random.fold_in(jax.random.fold_in(streams_of[5], part), 71), part),
        "values": scatter_about(part_splits[2], (LENGTH, KV_HEADS, HEAD_DIM), 1.0, 6.0, ((0, 4),)),
        "grad_out": scatter_about(part_splits[3], (LENGTH, HEADS, HEAD_DIM), 1.0, 6.0, ((0, 4), (1, 4))),
        "seg_ids": jnp.searchsorted(jnp.cumsum(ragged_sizes(part_splits[4], SEGS, LENGTH, SEG_MOST, 1)), jnp.arange(LENGTH), side="right").astype(jnp.int32),
    }


masked_score = -1.0e30


def reference(queries, keys, values, grad_out, seg_ids):
    softmax_scale = HEAD_DIM ** -0.5
    reach_rows = SPAN * TOK_DEV
    window_rows = reach_rows + TOK_DEV
    block_count = LENGTH // TOK_DEV
    key_pad = jnp.concatenate([jnp.zeros((reach_rows, KV_HEADS, HEAD_DIM), keys.dtype), keys], 0)
    value_pad = jnp.concatenate([jnp.zeros((reach_rows, KV_HEADS, HEAD_DIM), values.dtype), values], 0)
    seg_pad = jnp.concatenate([jnp.full((reach_rows,), -1, jnp.int32), seg_ids.astype(jnp.int32)], 0)
    pos_pad = jnp.arange(LENGTH + reach_rows, dtype=jnp.int32) - reach_rows

    def window(block_index):
        row_start = (block_index * TOK_DEV).astype(jnp.int32)
        query_block = lax.dynamic_slice_in_dim(queries, row_start, TOK_DEV, 0).astype(jnp.float32)
        query_block = query_block.reshape(TOK_DEV, KV_HEADS, GROUP, HEAD_DIM)
        key_window = lax.dynamic_slice_in_dim(key_pad, row_start, window_rows, 0).astype(jnp.float32)
        value_window = lax.dynamic_slice_in_dim(value_pad, row_start, window_rows, 0).astype(jnp.float32)
        key_seg = lax.dynamic_slice_in_dim(seg_pad, row_start, window_rows, 0)
        key_pos = lax.dynamic_slice_in_dim(pos_pad, row_start, window_rows, 0)
        query_seg = lax.dynamic_slice_in_dim(seg_ids.astype(jnp.int32), row_start, TOK_DEV, 0)
        query_pos = row_start + jnp.arange(TOK_DEV, dtype=jnp.int32)
        allowed = (key_pos[None, :] >= 0) & (key_pos[None, :] <= query_pos[:, None]) & (key_seg[None, :] == query_seg[:, None])
        raw_scores = jnp.einsum("tgjd,wgd->gjtw", query_block, key_window) * softmax_scale
        score_block = jnp.where(allowed[None, None], raw_scores, masked_score)
        return query_block, key_window, value_window, score_block

    def forward(block_index):
        unused_q, unused_k, value_window, score_block = window(block_index)
        row_max = jnp.max(score_block, -1, keepdims=True)
        log_total = row_max + jnp.log(jnp.sum(jnp.exp(score_block - row_max), -1, keepdims=True))
        weights = lax.optimization_barrier(jnp.exp(score_block - log_total).astype(jnp.bfloat16)).astype(jnp.float32)
        out_block = jnp.einsum("gjtw,wgd->tgjd", weights, value_window)
        return out_block.reshape(TOK_DEV, HEADS, HEAD_DIM).astype(jnp.bfloat16), log_total[..., 0]

    indices = jnp.arange(block_count, dtype=jnp.int32)
    out_blocks, log_totals = lax.map(forward, indices)
    attn_out = out_blocks.reshape(LENGTH, HEADS, HEAD_DIM)
    row_delta_all = jnp.sum(grad_out.astype(jnp.float32) * attn_out.astype(jnp.float32), -1)

    def backward(grad_pair, block_index):
        key_grads, value_grads = grad_pair
        query_block, key_window, value_window, score_block = window(block_index)
        row_start = (block_index * TOK_DEV).astype(jnp.int32)
        grad_grouped = lax.dynamic_slice_in_dim(grad_out, row_start, TOK_DEV, 0).astype(jnp.float32)
        grad_grouped = grad_grouped.reshape(TOK_DEV, KV_HEADS, GROUP, HEAD_DIM)
        row_delta = lax.dynamic_slice_in_dim(row_delta_all, row_start, TOK_DEV, 0)
        row_delta = row_delta.reshape(TOK_DEV, KV_HEADS, GROUP).transpose(1, 2, 0)
        log_total = log_totals[block_index]
        probs_full = jnp.exp(score_block - log_total[..., None])
        weights = lax.optimization_barrier(probs_full.astype(jnp.bfloat16)).astype(jnp.float32)
        grad_probs = jnp.einsum("tgjd,wgd->gjtw", grad_grouped, value_window)
        grad_scores = softmax_scale * probs_full * (grad_probs - row_delta[..., None])
        grad_scores = lax.optimization_barrier(grad_scores.astype(jnp.bfloat16)).astype(jnp.float32)
        query_term = jnp.einsum("gjtw,wgd->tgjd", grad_scores, key_window)
        key_term = jnp.einsum("gjtw,tgjd->wgd", grad_scores, query_block)
        value_term = jnp.einsum("gjtw,tgjd->wgd", weights, grad_grouped)
        key_grads = lax.dynamic_update_slice_in_dim(key_grads, lax.dynamic_slice_in_dim(key_grads, row_start, window_rows, 0) + key_term, row_start, 0)
        value_grads = lax.dynamic_update_slice_in_dim(value_grads, lax.dynamic_slice_in_dim(value_grads, row_start, window_rows, 0) + value_term, row_start, 0)
        return (key_grads, value_grads), query_term.reshape(TOK_DEV, HEADS, HEAD_DIM).astype(jnp.bfloat16)

    zero_grads = jnp.zeros((LENGTH + reach_rows, KV_HEADS, HEAD_DIM), jnp.float32)
    (key_grads, value_grads), query_blocks = lax.scan(backward, (zero_grads, zero_grads), indices)
    grad_q = query_blocks.reshape(LENGTH, HEADS, HEAD_DIM)
    grad_k = key_grads[reach_rows:].astype(jnp.bfloat16)
    grad_v = value_grads[reach_rows:].astype(jnp.bfloat16)
    return (attn_out, grad_q, grad_k, grad_v)
```

```python
import functools
import math

import jax
import jax.numpy as jnp
from jax import lax
from jax.experimental import pallas as pl
from jax.experimental.pallas import tpu as pltpu
from jax.sharding import PartitionSpec as P

GROUP = 8
MASKED = -1e30
MESH = pl.DeviceIdType.MESH


def dot(a, b, ca, cb):
    return lax.dot_general(
        a, b, (((ca,), (cb,)), ((), ())), preferred_element_type=jnp.float32
    )


def kernel(
    cfg, q_ref, do_ref, kv_ref, segrow_ref, segq_ref,
    out_ref, dq_ref, grads_ref,
    kv_buf, seg_buf, kcat, vcat, segcat, p_buf, ds_buf, dkcat, dvcat,
    back_send, back_recv, gather, share_recv,
    kv_ssem, kv_rsem, seg_ssem, seg_rsem, b_ssem, b_rsem, g_ssem, g_rsem, h_ssem, h_rsem,
):
    n_in, reach, n_out, kvl, gh, share, tok = cfg
    head_dim = q_ref.shape[-1]
    half = tok // 2
    scale = head_dim ** (-0.5)
    width = half + half + tok * (reach - 1)
    pos = lax.axis_index("inner")
    outer = lax.axis_index("outer")
    core = lax.axis_index("heads")

    barrier = pltpu.get_barrier_semaphore()

    @pl.when(pos > 0)
    def _():
        pl.semaphore_signal(barrier, inc=1, device_id={"inner": pos - 1}, device_id_type=MESH)

    @pl.when(pos < n_in - 1)
    def _():
        pl.semaphore_signal(barrier, inc=1, device_id={"inner": pos + 1}, device_id_type=MESH)

    pl.semaphore_signal(barrier, inc=1, device_id={"heads": 1 - core}, device_id_type=MESH)
    for o in range(1, n_out):
        pl.semaphore_signal(
            barrier, inc=1, device_id={"outer": lax.rem(outer + o, n_out)}, device_id_type=MESH
        )
    ends = jnp.where(pos > 0, 1, 0) + jnp.where(pos < n_in - 1, 1, 0)
    pl.semaphore_wait(barrier, ends + n_out)

    def kv_copy(g, d):
        src = kv_ref.at[g] if d == 1 else kv_buf.at[g, d - 2]
        return pltpu.make_async_remote_copy(
            src_ref=src, dst_ref=kv_buf.at[g, d - 1],
            send_sem=kv_ssem.at[g, d - 1], recv_sem=kv_rsem.at[g, d - 1],
            device_id={"inner": pos + 1}, device_id_type=MESH,
        )

    def seg_copy(d):
        src = segrow_ref if d == 1 else seg_buf.at[d - 2]
        return pltpu.make_async_remote_copy(
            src_ref=src, dst_ref=seg_buf.at[d - 1],
            send_sem=seg_ssem.at[d - 1], recv_sem=seg_rsem.at[d - 1],
            device_id={"inner": pos + 1}, device_id_type=MESH,
        )

    def sends(d):
        return (pos + 1 < n_in) & (pos >= d - 1)

    def back_receives(d):
        return (pos + 1 < n_in) & (pos + 1 >= d)

    def start_hop(d):
        @pl.when(sends(d))
        def _():
            seg_copy(d).start()
            for g in range(kvl):
                kv_copy(g, d).start()

    for d in range(1, reach + 1):
        @pl.when(pos < d)
        def _():
            seg_buf[d - 1] = jnp.full(seg_buf.shape[1:], -1, jnp.int32)
            for g in range(kvl):
                kv_buf[g, d - 1] = jnp.zeros(kv_buf.shape[2:], kv_buf.dtype)

        @pl.when(jnp.logical_not(back_receives(d)))
        def _():
            for g in range(kvl):
                back_recv[g, d - 1] = jnp.zeros(back_recv.shape[2:], back_recv.dtype)

    start_hop(1)
    for d in range(1, reach + 1):
        @pl.when(pos >= d)
        def _():
            seg_copy(d).wait_recv()
            kv_copy(0, d).wait_recv()
        if d < reach:
            @pl.when(sends(d + 1))
            def _():
                seg_copy(d + 1).start()
                kv_copy(0, d + 1).start()
            for g in range(1, kvl):
                @pl.when(pos >= d)
                def _():
                    kv_copy(g, d).wait_recv()

                @pl.when(sends(d + 1))
                def _():
                    kv_copy(g, d + 1).start()

    def block(g, c, d, rows):
        if d == 0:
            return kv_ref[g, c, rows, :]
        return kv_buf[g, d - 1, c, rows, :]

    low, high = slice(0, half), slice(half, tok)
    mixes = (low, high)

    for hf in range(2):
        rest = high if hf == 0 else low
        far = reach if hf == 0 else 0
        seg0 = segrow_ref[:, mixes[hf]]
        segr = seg_buf[reach - 1, :, mixes[hf]]
        segcat[hf, :, 0:half] = seg0
        segcat[hf, :, half:tok] = segr
        segcat[hf, :, tok:tok + half] = segrow_ref[:, rest] if far == 0 else seg_buf[reach - 1, :, rest]
        for d in range(1, reach):
            at = tok + half + (d - 1) * tok
            segcat[hf, :, at:at + tok] = seg_buf[d - 1]

    rows_half = half * gh
    rows = min(512, rows_half)
    chunks = rows_half // rows
    tokens = rows // gh

    def compute(g, hf):
        rest = high if hf == 0 else low
        far = reach if hf == 0 else 0
        for c, cat in ((0, kcat), (1, vcat)):
            cat[0:half, :] = block(g, c, 0, mixes[hf])
            cat[half:tok, :] = block(g, c, reach, mixes[hf])
            cat[tok:tok + half, :] = block(g, c, far, rest)
            for d in range(1, reach):
                at = tok + half + (d - 1) * tok
                cat[at:at + tok, :] = block(g, c, d, slice(None))

        def chunk(i, carry):
            local = pl.ds(pl.multiple_of(i * rows, rows), rows)
            where = pl.ds(pl.multiple_of(hf * rows_half + i * rows, rows), rows)
            q = q_ref[g, where, :]
            do = do_ref[g, where, :]
            row_tok = lax.broadcasted_iota(jnp.int32, (rows, half), 0) // gh + i * tokens
            causal = lax.broadcasted_iota(jnp.int32, (rows, half), 1) <= row_tok
            seg_q = segq_ref[where, :]

            def merge(full):
                return [jnp.where(causal, full[:, 0:half], full[:, half:tok])] + [
                    full[:, at:at + half] for at in range(tok, width + half, half)
                ]

            segs = [segcat[hf, 0:1, at:at + half] for at in range(0, width + half, half)]
            seg_k = [jnp.where(causal, segs[0], segs[1])] + segs[2:]
            scores = merge(dot(q, kcat[...], 1, 1))
            scores = [jnp.where(k == seg_q, s, MASKED) for k, s in zip(seg_k, scores)]
            top = jnp.max(functools.reduce(jnp.maximum, scores), 1, keepdims=True)
            es = [jnp.exp2((s - top) * (scale * math.log2(math.e))) for s in scores]
            total = jnp.sum(functools.reduce(jnp.add, es), 1, keepdims=True)
            inv = 1.0 / total
            ps = [e * inv for e in es]

            def spread(parts):
                own = jnp.where(causal, parts[0], 0.0)
                other = jnp.where(causal, 0.0, parts[0])
                return jnp.concatenate(
                    [x.astype(jnp.bfloat16) for x in [own, other] + parts[1:]], 1
                )

            pb = spread(ps)
            p_buf[local, :] = pb
            ob = dot(pb, vcat[...], 1, 0).astype(jnp.bfloat16)
            out_ref[g, where, :] = ob
            delta = jnp.sum(do.astype(jnp.float32) * ob.astype(jnp.float32), 1, keepdims=True)
            dps = merge(dot(do, vcat[...], 1, 1))
            dsb = spread([(p * scale) * (dp - delta) for p, dp in zip(ps, dps)])
            ds_buf[local, :] = dsb
            dq_ref[g, where, :] = dot(dsb, kcat[...], 1, 0).astype(jnp.bfloat16)
            return carry

        lax.fori_loop(0, chunks, chunk, 0)
        where = pl.ds(hf * rows_half, rows_half)
        dkcat[g, hf] = dot(ds_buf[...], q_ref[g, where, :], 0, 0)
        dvcat[g, hf] = dot(p_buf[...], do_ref[g, where, :], 0, 0)

    def partial(g, c, d, part):
        cat = (dkcat if c == 0 else dvcat).at[g]
        if d == 0:
            if part == 0:
                return cat[0, 0:half, :] + cat[1, tok:tok + half, :]
            return cat[1, 0:half, :]
        if d == reach:
            if part == 0:
                return cat[0, half:tok, :]
            return cat[1, half:tok, :] + cat[0, tok:tok + half, :]
        at = tok + half + (d - 1) * tok + part * half
        return cat[0, at:at + half, :] + cat[1, at:at + half, :]

    def back_copy(g, d):
        return pltpu.make_async_remote_copy(
            src_ref=back_send.at[g, d - 1], dst_ref=back_recv.at[g, d - 1],
            send_sem=b_ssem.at[g, d - 1], recv_sem=b_rsem.at[g, d - 1],
            device_id={"inner": pos - 1}, device_id_type=MESH,
        )

    def summed(ref, g, d):
        for c in range(2):
            for part in range(2):
                term = partial(g, c, d, part)
                if d < reach:
                    term = term + back_recv[g, d, c, mixes[part], :].astype(jnp.float32)
                ref[c, mixes[part], :] = term.astype(ref.dtype)

    slot = (outer * 2 + core) * kvl // share

    def final(g):
        return gather.at[slot + g]

    def outer_copy(g, o):
        return pltpu.make_async_remote_copy(
            src_ref=final(g), dst_ref=final(g),
            send_sem=g_ssem.at[g, o - 1], recv_sem=g_rsem.at[g, o - 1],
            device_id={"outer": lax.rem(outer + o, n_out)}, device_id_type=MESH,
        )

    def sibling_copy(g, o):
        src_outer = lax.rem(outer - o + n_out, n_out)
        at = gather.at[(src_outer * 2 + core) * kvl // share + g]
        return pltpu.make_async_remote_copy(
            src_ref=at, dst_ref=at,
            send_sem=h_ssem.at[g, o], recv_sem=h_rsem.at[g, o],
            device_id={"heads": 1 - core}, device_id_type=MESH,
        )

    def share_copy(g):
        return pltpu.make_async_remote_copy(
            src_ref=final(g), dst_ref=share_recv.at[g],
            send_sem=h_ssem.at[g, 0], recv_sem=h_rsem.at[g, 0],
            device_id={"heads": 1 - core}, device_id_type=MESH,
        )

    def chain_step(g, d):
        if d < reach:
            @pl.when(back_receives(d + 1))
            def _():
                back_copy(g, d + 1).wait_recv()
        if d > 0:
            summed(back_send.at[g, d - 1], g, d)

            @pl.when(pos >= d)
            def _():
                back_copy(g, d).start()
            return
        summed(final(g), g, 0)
        if share > 1:
            copy = share_copy(g)
            copy.start()
            copy.wait()
            final(g)[...] = (
                final(g)[...].astype(jnp.float32) + share_recv[g].astype(jnp.float32)
            ).astype(gather.dtype)
        else:
            sibling_copy(g, 0).start()
        for o in range(1, n_out):
            outer_copy(g, o).start()

    for g in range(kvl):
        if g > 0:
            @pl.when(pos >= reach)
            def _():
                kv_copy(g, reach).wait_recv()
        for hf in range(2):
            compute(g, hf)
            if g > 0 and hf == 0:
                for d in range(reach - 1, 0, -1):
                    chain_step(g - 1, d)
        if g > 0:
            chain_step(g - 1, 0)
        chain_step(g, reach)
    for d in range(reach - 1, -1, -1):
        chain_step(kvl - 1, d)

    for g in range(kvl):
        for o in range(1, n_out):
            outer_copy(g, o).wait_recv()
            if share == 1:
                sibling_copy(g, o).start()
    if share == 1:
        for g in range(kvl):
            for o in range(n_out):
                sibling_copy(g, o).wait_recv()
    grads_ref[...] = gather[...]

    for d in range(1, reach + 1):
        @pl.when(sends(d))
        def _():
            seg_copy(d).wait_send()
            for g in range(kvl):
                kv_copy(g, d).wait_send()

        @pl.when(pos >= d)
        def _():
            for g in range(kvl):
                back_copy(g, d).wait_send()
    for g in range(kvl):
        for o in range(1, n_out):
            outer_copy(g, o).wait_send()
        if share == 1:
            for o in range(n_out):
                sibling_copy(g, o).wait_send()


def shards(queries, keys, values, grad_out, seg_ids):
    tok, heads, depth = queries.shape
    kv_total = keys.shape[1]
    gh = min(GROUP, heads)
    kvl = heads // gh
    share = GROUP // gh
    n_in, n_out = lax.axis_size("inner"), lax.axis_size("outer")
    reach = n_in // 2
    rows = tok * gh
    width = tok + (tok // 2) + tok * (reach - 1)
    slot = lax.axis_index(("outer", "heads")) * heads // GROUP
    wire = jnp.bfloat16 if reach <= 2 else jnp.float32

    def grouped(x):
        return x.reshape(tok, kvl, gh, depth).transpose(1, 0, 2, 3).reshape(kvl, rows, depth)

    def ungrouped(x):
        return x.reshape(kvl, tok, gh, depth).transpose(1, 0, 2, 3).reshape(tok, heads, depth)

    kv_own = jnp.stack(
        [lax.dynamic_slice_in_dim(x, slot, kvl, 1).transpose(1, 0, 2) for x in (keys, values)], 1
    )
    seg_row = jnp.broadcast_to(seg_ids[None, :], (8, tok))
    seg_q = jnp.broadcast_to(jnp.repeat(seg_ids, gh)[:, None], (rows, tok // 2))
    bf, f32 = jnp.bfloat16, jnp.float32
    dma = pltpu.SemaphoreType.DMA
    vmem = pl.BlockSpec(memory_space=pltpu.VMEM)
    out, dq, grads = pl.pallas_call(
        functools.partial(kernel, (n_in, reach, n_out, kvl, gh, share, tok)),
        out_shape=(
            jax.ShapeDtypeStruct((kvl, rows, depth), bf),
            jax.ShapeDtypeStruct((kvl, rows, depth), bf),
            jax.ShapeDtypeStruct((kv_total, 2, tok, depth), bf),
        ),
        in_specs=[vmem] * 5,
        out_specs=(vmem,) * 3,
        scratch_shapes=[
            pltpu.VMEM((kvl, reach, 2, tok, depth), bf),
            pltpu.VMEM((reach, 8, tok), jnp.int32),
            pltpu.VMEM((width, depth), bf),
            pltpu.VMEM((width, depth), bf),
            pltpu.VMEM((2, 8, width), jnp.int32),
            pltpu.VMEM((rows // 2, width), bf),
            pltpu.VMEM((rows // 2, width), bf),
            pltpu.VMEM((kvl, 2, width, depth), f32),
            pltpu.VMEM((kvl, 2, width, depth), f32),
            pltpu.VMEM((kvl, reach, 2, tok, depth), wire),
            pltpu.VMEM((kvl, reach, 2, tok, depth), wire),
            pltpu.VMEM((kv_total, 2, tok, depth), bf),
            pltpu.VMEM((kvl, 2, tok, depth), bf),
            dma((kvl, reach)), dma((kvl, reach)),
            dma((reach,)), dma((reach,)),
            dma((kvl, reach)), dma((kvl, reach)),
            dma((kvl, n_out)), dma((kvl, n_out)),
            dma((kvl, n_out)), dma((kvl, n_out)),
        ],
        compiler_params=pltpu.CompilerParams(
            collective_id=0, has_side_effects=True, vmem_limit_bytes=48 * 2**20
        ),
    )(grouped(queries), grouped(grad_out), kv_own, seg_row, seg_q)
    return (
        ungrouped(out),
        ungrouped(dq),
        grads[:, 0].transpose(1, 0, 2),
        grads[:, 1].transpose(1, 0, 2),
    )


def solution(mesh):
    act = P(("groups", "inner"), ("outer", "heads"), None)
    kv = P(("groups", "inner"), None, None)
    return jax.shard_map(
        shards,
        mesh=mesh,
        in_specs=(act, kv, kv, act, P(("groups", "inner"))),
        out_specs=(act, act, kv, kv),
        check_vma=False,
    )
```

```python
import functools
import math

import jax
import jax.numpy as jnp
from jax import lax
from jax.experimental import pallas as pl
from jax.experimental.pallas import tpu as pltpu
from jax.sharding import PartitionSpec as P

GROUP = 8
MASKED = -1e30
MESH = pl.DeviceIdType.MESH


def dot(a, b, ca, cb):
    return lax.dot_general(
        a, b, (((ca,), (cb,)), ((), ())), preferred_element_type=jnp.float32
    )


def kernel(
    cfg, q_ref, do_ref, key_ref, value_ref, segrow_ref,
    out_ref, dq_ref, grads_ref,
    kv_ref, segq_ref, flat, kv_buf, seg_buf, kcat, vcat, segcat, p_buf, ds_buf, dkcat, dvcat,
    back_send, back_recv, gather, share_recv,
    kv_ssem, kv_rsem, seg_ssem, seg_rsem, b_ssem, b_rsem, g_ssem, g_rsem, h_ssem, h_rsem,
):
    n_in, reach, n_out, kvl, gh, share, tok = cfg
    head_dim = q_ref.shape[-1]
    half = tok // 2
    scale = head_dim ** (-0.5)
    width = half + half + tok * (reach - 1)
    pos = lax.axis_index("inner")
    outer = lax.axis_index("outer")
    core = lax.axis_index("heads")
    slot = (outer * 2 + core) * kvl // share

    for c, ref in ((0, key_ref), (1, value_ref)):
        flat[...] = ref[...].astype(jnp.float32).reshape(flat.shape)
        for g in range(kvl):
            kv_ref[g, c] = flat[pl.ds(slot + g, tok, stride=ref.shape[1]), :].astype(kv_ref.dtype)

    barrier = pltpu.get_barrier_semaphore()

    @pl.when(pos > 0)
    def _():
        pl.semaphore_signal(barrier, inc=1, device_id={"inner": pos - 1}, device_id_type=MESH)

    @pl.when(pos < n_in - 1)
    def _():
        pl.semaphore_signal(barrier, inc=1, device_id={"inner": pos + 1}, device_id_type=MESH)

    pl.semaphore_signal(barrier, inc=1, device_id={"heads": 1 - core}, device_id_type=MESH)
    for o in range(1, n_out):
        pl.semaphore_signal(
            barrier, inc=1, device_id={"outer": lax.rem(outer + o, n_out)}, device_id_type=MESH
        )
    ends = jnp.where(pos > 0, 1, 0) + jnp.where(pos < n_in - 1, 1, 0)
    pl.semaphore_wait(barrier, ends + n_out)

    def kv_copy(g, c, d):
        src = kv_ref.at[g, c] if d == 1 else kv_buf.at[g, d - 2, c]
        return pltpu.make_async_remote_copy(
            src_ref=src, dst_ref=kv_buf.at[g, d - 1, c],
            send_sem=kv_ssem.at[g, d - 1, c], recv_sem=kv_rsem.at[g, d - 1, c],
            device_id={"inner": pos + 1}, device_id_type=MESH,
        )

    def seg_copy(d):
        src = segrow_ref if d == 1 else seg_buf.at[d - 2]
        return pltpu.make_async_remote_copy(
            src_ref=src, dst_ref=seg_buf.at[d - 1],
            send_sem=seg_ssem.at[d - 1], recv_sem=seg_rsem.at[d - 1],
            device_id={"inner": pos + 1}, device_id_type=MESH,
        )

    def sends(d):
        return (pos + 1 < n_in) & (pos >= d - 1)

    def back_receives(d):
        return (pos + 1 < n_in) & (pos + 1 >= d)

    def start_own(g):
        @pl.when(sends(1))
        def _():
            for c in range(2):
                kv_copy(g, c, 1).start()

    def forward(g):
        for d in range(1, reach):
            for c in range(2):
                @pl.when(pos >= d)
                def _():
                    kv_copy(g, c, d).wait_recv()

                @pl.when(sends(d + 1))
                def _():
                    kv_copy(g, c, d + 1).start()

    def farthest(g):
        @pl.when(pos >= reach)
        def _():
            for c in range(2):
                kv_copy(g, c, reach).wait_recv()

    start_own(0)

    @pl.when(sends(1))
    def _():
        seg_copy(1).start()

    for d in range(1, reach + 1):
        @pl.when(pos < d)
        def _():
            seg_buf[d - 1] = jnp.full(seg_buf.shape[1:], -1, jnp.int32)
            for g in range(kvl):
                kv_buf[g, d - 1] = jnp.zeros(kv_buf.shape[2:], kv_buf.dtype)

        @pl.when(jnp.logical_not(back_receives(d)))
        def _():
            for g in range(kvl):
                back_recv[g, d - 1] = jnp.zeros(back_recv.shape[2:], back_recv.dtype)

    seg_col = jnp.transpose(jnp.broadcast_to(segrow_ref[0:1, :], (half, tok)))
    for j in range(gh):
        segq_ref[pl.ds(j, tok, stride=gh), :] = seg_col
    for d in range(1, reach + 1):
        @pl.when(pos >= d)
        def _():
            seg_copy(d).wait_recv()

        if d < reach:
            @pl.when(sends(d + 1))
            def _():
                seg_copy(d + 1).start()
    forward(0)
    for g in range(1, kvl):
        start_own(g)
    farthest(0)

    def block(g, c, d, rows):
        if d == 0:
            return kv_ref[g, c, rows, :]
        return kv_buf[g, d - 1, c, rows, :]

    low, high = slice(0, half), slice(half, tok)
    mixes = (low, high)

    for hf in range(2):
        rest = high if hf == 0 else low
        far = reach if hf == 0 else 0
        seg0 = segrow_ref[:, mixes[hf]]
        segr = seg_buf[reach - 1, :, mixes[hf]]
        segcat[hf, :, 0:half] = seg0
        segcat[hf, :, half:tok] = segr
        segcat[hf, :, tok:tok + half] = segrow_ref[:, rest] if far == 0 else seg_buf[reach - 1, :, rest]
        for d in range(1, reach):
            at = tok + half + (d - 1) * tok
            segcat[hf, :, at:at + tok] = seg_buf[d - 1]

    rows_half = half * gh
    rows = min(512, rows_half)
    chunks = rows_half // rows
    tokens = rows // gh

    def compute(g, hf):
        rest = high if hf == 0 else low
        far = reach if hf == 0 else 0
        for c, cat in ((0, kcat), (1, vcat)):
            cat[0:half, :] = block(g, c, 0, mixes[hf])
            cat[half:tok, :] = block(g, c, reach, mixes[hf])
            cat[tok:tok + half, :] = block(g, c, far, rest)
            for d in range(1, reach):
                at = tok + half + (d - 1) * tok
                cat[at:at + tok, :] = block(g, c, d, slice(None))

        def chunk(i, carry):
            local = pl.ds(pl.multiple_of(i * rows, rows), rows)
            where = pl.ds(pl.multiple_of(hf * rows_half + i * rows, rows), rows)
            q = q_ref[g, where, :]
            do = do_ref[g, where, :]
            row_tok = lax.broadcasted_iota(jnp.int32, (rows, half), 0) // gh + i * tokens
            causal = lax.broadcasted_iota(jnp.int32, (rows, half), 1) <= row_tok
            seg_q = segq_ref[where, :]

            def merge(full):
                return [jnp.where(causal, full[:, 0:half], full[:, half:tok])] + [
                    full[:, at:at + half] for at in range(tok, width + half, half)
                ]

            segs = [segcat[hf, 0:1, at:at + half] for at in range(0, width + half, half)]
            seg_k = [jnp.where(causal, segs[0], segs[1])] + segs[2:]
            scores = merge(dot(q, kcat[...], 1, 1))
            scores = [jnp.where(k == seg_q, s, MASKED) for k, s in zip(seg_k, scores)]
            top = jnp.max(functools.reduce(jnp.maximum, scores), 1, keepdims=True)
            es = [jnp.exp2((s - top) * (scale * math.log2(math.e))) for s in scores]
            total = jnp.sum(functools.reduce(jnp.add, es), 1, keepdims=True)
            inv = 1.0 / total
            ps = [e * inv for e in es]

            def spread(parts):
                own = jnp.where(causal, parts[0], 0.0)
                other = jnp.where(causal, 0.0, parts[0])
                return jnp.concatenate(
                    [x.astype(jnp.bfloat16) for x in [own, other] + parts[1:]], 1
                )

            pb = spread(ps)
            p_buf[local, :] = pb
            ob = dot(pb, vcat[...], 1, 0).astype(jnp.bfloat16)
            out_ref[g, where, :] = ob
            delta = jnp.sum(do.astype(jnp.float32) * ob.astype(jnp.float32), 1, keepdims=True)
            dps = merge(dot(do, vcat[...], 1, 1))
            dsb = spread([(p * scale) * (dp - delta) for p, dp in zip(ps, dps)])
            ds_buf[local, :] = dsb
            dq_ref[g, where, :] = dot(dsb, kcat[...], 1, 0).astype(jnp.bfloat16)
            return carry

        lax.fori_loop(0, chunks, chunk, 0)

    def weigh(g, hf, c):
        where = pl.ds(hf * rows_half, rows_half)
        if c == 0:
            dkcat[g, hf] = dot(ds_buf[...], q_ref[g, where, :], 0, 0)
        else:
            dvcat[g, hf] = dot(p_buf[...], do_ref[g, where, :], 0, 0)

    def partial(g, c, d, part):
        cat = (dkcat if c == 0 else dvcat).at[g]
        if d == 0:
            if part == 0:
                return cat[0, 0:half, :] + cat[1, tok:tok + half, :]
            return cat[1, 0:half, :]
        if d == reach:
            if part == 0:
                return cat[0, half:tok, :]
            return cat[1, half:tok, :] + cat[0, tok:tok + half, :]
        at = tok + half + (d - 1) * tok + part * half
        return cat[0, at:at + half, :] + cat[1, at:at + half, :]

    def back_copy(g, d, c, part):
        at = (g, d - 1, c, mixes[part])
        return pltpu.make_async_remote_copy(
            src_ref=back_send.at[at], dst_ref=back_recv.at[at],
            send_sem=b_ssem.at[g, d - 1, c, part], recv_sem=b_rsem.at[g, d - 1, c, part],
            device_id={"inner": pos - 1}, device_id_type=MESH,
        )

    def summed(g, d, c, part):
        term = partial(g, c, d, part)
        if d < reach:
            term = term + back_recv[g, d, c, mixes[part], :].astype(jnp.float32)
        return term

    def outer_copy(g, o, c, part):
        at = gather.at[slot + g, c, mixes[part]]
        return pltpu.make_async_remote_copy(
            src_ref=at, dst_ref=at,
            send_sem=g_ssem.at[g, o - 1, c, part], recv_sem=g_rsem.at[g, o - 1, c, part],
            device_id={"outer": lax.rem(outer + o, n_out)}, device_id_type=MESH,
        )

    def sibling_copy(g, o, c, part):
        src_outer = lax.rem(outer - o + n_out, n_out)
        at = gather.at[(src_outer * 2 + core) * kvl // share + g, c, mixes[part]]
        return pltpu.make_async_remote_copy(
            src_ref=at, dst_ref=at,
            send_sem=h_ssem.at[g, o, c, part], recv_sem=h_rsem.at[g, o, c, part],
            device_id={"heads": 1 - core}, device_id_type=MESH,
        )

    def share_copy(g, c, part):
        return pltpu.make_async_remote_copy(
            src_ref=gather.at[slot + g, c, mixes[part]], dst_ref=share_recv.at[g, c, mixes[part]],
            send_sem=h_ssem.at[g, 0, c, part], recv_sem=h_rsem.at[g, 0, c, part],
            device_id={"heads": 1 - core}, device_id_type=MESH,
        )

    pieces = [(c, part) for c in (1, 0) for part in (0, 1)]

    def step(g, d, c, part):
        if d < reach:
            @pl.when(back_receives(d + 1))
            def _():
                back_copy(g, d + 1, c, part).wait_recv()
        if d > 0:
            back_send[g, d - 1, c, mixes[part], :] = summed(g, d, c, part).astype(back_send.dtype)

            @pl.when(pos >= d)
            def _():
                back_copy(g, d, c, part).start()
            return
        own = gather.at[slot + g, c, mixes[part]]
        own[...] = summed(g, 0, c, part).astype(gather.dtype)
        if share > 1:
            copy = share_copy(g, c, part)
            copy.start()
            copy.wait()
            got = share_recv[g, c, mixes[part], :].astype(jnp.float32)
            own[...] = (own[...].astype(jnp.float32) + got).astype(gather.dtype)
        for o in range(1, n_out):
            outer_copy(g, o, c, part).start()
        if share == 1:
            sibling_copy(g, 0, c, part).start()

    def arrive(g):
        for c, part in pieces:
            for o in range(1, n_out):
                outer_copy(g, o, c, part).wait_recv()
                if share == 1:
                    sibling_copy(g, o, c, part).start()

    for g in range(kvl):
        if g > 0:
            farthest(g)
        compute(g, 0)
        for c in (1, 0):
            weigh(g, 0, c)
            step(g, reach, c, 0)
        if g + 1 < kvl:
            forward(g + 1)
        if g > 0:
            for d in range(reach - 1, 0, -1):
                for c, part in pieces:
                    step(g - 1, d, c, part)
        compute(g, 1)
        for c in (1, 0):
            weigh(g, 1, c)
            step(g, reach, c, 1)
        if g > 0:
            for c, part in pieces:
                step(g - 1, 0, c, part)
    for d in range(reach - 1, -1, -1):
        for c, part in pieces:
            step(kvl - 1, d, c, part)
    for g in range(kvl):
        arrive(g)
    if share == 1:
        for g in range(kvl):
            for c, part in pieces:
                for o in range(n_out):
                    sibling_copy(g, o, c, part).wait_recv()
    grads_ref[...] = gather[...]

    for d in range(1, reach + 1):
        @pl.when(sends(d))
        def _():
            seg_copy(d).wait_send()
            for g in range(kvl):
                for c in range(2):
                    kv_copy(g, c, d).wait_send()

        @pl.when(pos >= d)
        def _():
            for g in range(kvl):
                for c, part in pieces:
                    back_copy(g, d, c, part).wait_send()
    for g in range(kvl):
        for c, part in pieces:
            for o in range(1, n_out):
                outer_copy(g, o, c, part).wait_send()
            if share == 1:
                for o in range(n_out):
                    sibling_copy(g, o, c, part).wait_send()


def shards(queries, keys, values, grad_out, seg_ids):
    tok, heads, depth = queries.shape
    kv_total = keys.shape[1]
    gh = min(GROUP, heads)
    kvl = heads // gh
    share = GROUP // gh
    n_in, n_out = lax.axis_size("inner"), lax.axis_size("outer")
    reach = n_in // 2
    rows = tok * gh
    width = tok + (tok // 2) + tok * (reach - 1)
    wire = jnp.bfloat16 if reach <= 2 else jnp.float32

    def grouped(x):
        return x.reshape(tok, kvl, gh, depth).transpose(1, 0, 2, 3).reshape(kvl, rows, depth)

    def ungrouped(x):
        return x.reshape(kvl, tok, gh, depth).transpose(1, 0, 2, 3).reshape(tok, heads, depth)

    seg_row = jnp.broadcast_to(seg_ids[None, :], (8, tok))
    bf, f32 = jnp.bfloat16, jnp.float32
    dma = pltpu.SemaphoreType.DMA
    vmem = pl.BlockSpec(memory_space=pltpu.VMEM)
    out, dq, grads = pl.pallas_call(
        functools.partial(kernel, (n_in, reach, n_out, kvl, gh, share, tok)),
        out_shape=(
            jax.ShapeDtypeStruct((kvl, rows, depth), bf),
            jax.ShapeDtypeStruct((kvl, rows, depth), bf),
            jax.ShapeDtypeStruct((kv_total, 2, tok, depth), bf),
        ),
        in_specs=[vmem] * 5,
        out_specs=(vmem,) * 3,
        scratch_shapes=[
            pltpu.VMEM((kvl, 2, tok, depth), bf),
            pltpu.VMEM((rows, tok // 2), jnp.int32),
            pltpu.VMEM((tok * kv_total, depth), f32),
            pltpu.VMEM((kvl, reach, 2, tok, depth), bf),
            pltpu.VMEM((reach, 8, tok), jnp.int32),
            pltpu.VMEM((width, depth), bf),
            pltpu.VMEM((width, depth), bf),
            pltpu.VMEM((2, 8, width), jnp.int32),
            pltpu.VMEM((rows // 2, width), bf),
            pltpu.VMEM((rows // 2, width), bf),
            pltpu.VMEM((kvl, 2, width, depth), f32),
            pltpu.VMEM((kvl, 2, width, depth), f32),
            pltpu.VMEM((kvl, reach, 2, tok, depth), wire),
            pltpu.VMEM((kvl, reach, 2, tok, depth), wire),
            pltpu.VMEM((kv_total, 2, tok, depth), bf),
            pltpu.VMEM((kvl, 2, tok, depth), bf),
            dma((kvl, reach, 2)), dma((kvl, reach, 2)),
            dma((reach,)), dma((reach,)),
            dma((kvl, reach, 2, 2)), dma((kvl, reach, 2, 2)),
            dma((kvl, n_out, 2, 2)), dma((kvl, n_out, 2, 2)),
            dma((kvl, n_out, 2, 2)), dma((kvl, n_out, 2, 2)),
        ],
        compiler_params=pltpu.CompilerParams(
            collective_id=0, has_side_effects=True, vmem_limit_bytes=48 * 2**20
        ),
    )(grouped(queries), grouped(grad_out), keys, values, seg_row)
    return (
        ungrouped(out),
        ungrouped(dq),
        grads[:, 0].transpose(1, 0, 2),
        grads[:, 1].transpose(1, 0, 2),
    )


def solution(mesh):
    act = P(("groups", "inner"), ("outer", "heads"), None)
    kv = P(("groups", "inner"), None, None)
    return jax.shard_map(
        shards,
        mesh=mesh,
        in_specs=(act, kv, kv, act, P(("groups", "inner"))),
        out_specs=(act, act, kv, kv),
        check_vma=False,
    )
```

```python
import functools
import math

import jax
import jax.numpy as jnp
from jax import lax
from jax.experimental import pallas as pl
from jax.experimental.pallas import tpu as pltpu
from jax.sharding import PartitionSpec as P

GROUP = 8
MASKED = -1e30
MESH = pl.DeviceIdType.MESH


def dot(a, b, ca, cb):
    return lax.dot_general(
        a, b, (((ca,), (cb,)), ((), ())), preferred_element_type=jnp.float32
    )


def kernel(
    cfg, q_arg, do_arg, key_ref, value_ref, seg_arg,
    out_res, dq_res, dk_res, dv_res,
    q_in, do_in, q_ref, do_ref, out_ref, dq_ref, segrow_ref, in_sem, kv_ref, segq_ref, flat, kv_buf, seg_buf, kcat, vcat, segcat, p_buf, ds_buf, dkcat, dvcat,
    back_send, back_recv, gather, share_recv,
    kv_ssem, kv_rsem, seg_ssem, seg_rsem, b_ssem, b_rsem, g_ssem, g_rsem, h_ssem, h_rsem,
):
    n_in, reach, n_out, kvl, gh, share, tok = cfg
    head_dim = q_ref.shape[-1]
    half = tok // 2
    native = gh % 8 == 0
    scale = head_dim ** (-0.5)
    width = half + half + tok * (reach - 1)
    pos = lax.axis_index("inner")
    outer = lax.axis_index("outer")
    core = lax.axis_index("heads")
    slot = (outer * 2 + core) * kvl // share

    loads = [
        pltpu.make_async_copy(arg, buf, in_sem.at[i])
        for i, (arg, buf) in enumerate(((q_arg, q_in), (do_arg, do_in)))
    ]
    for load in loads:
        load.start()
    segrow_ref[...] = jnp.broadcast_to(seg_arg[...], segrow_ref.shape)
    for c, ref in ((0, key_ref), (1, value_ref)):
        flat[c] = ref[...].astype(jnp.float32).reshape(flat.shape[1:])
        for g in range(kvl):
            kv_ref[g, c] = flat[c, pl.ds(slot + g, tok, stride=ref.shape[1]), :].astype(kv_ref.dtype)

    barrier = pltpu.get_barrier_semaphore()

    @pl.when(pos > 0)
    def _():
        pl.semaphore_signal(barrier, inc=1, device_id={"inner": pos - 1}, device_id_type=MESH)

    @pl.when(pos < n_in - 1)
    def _():
        pl.semaphore_signal(barrier, inc=1, device_id={"inner": pos + 1}, device_id_type=MESH)

    pl.semaphore_signal(barrier, inc=1, device_id={"heads": 1 - core}, device_id_type=MESH)
    for o in range(1, n_out):
        pl.semaphore_signal(
            barrier, inc=1, device_id={"outer": lax.rem(outer + o, n_out)}, device_id_type=MESH
        )
    ends = jnp.where(pos > 0, 1, 0) + jnp.where(pos < n_in - 1, 1, 0)
    pl.semaphore_wait(barrier, ends + n_out)

    def kv_copy(g, c, d):
        src = kv_ref.at[g, c] if d == 1 else kv_buf.at[g, d - 2, c]
        return pltpu.make_async_remote_copy(
            src_ref=src, dst_ref=kv_buf.at[g, d - 1, c],
            send_sem=kv_ssem.at[g, d - 1, c], recv_sem=kv_rsem.at[g, d - 1, c],
            device_id={"inner": pos + 1}, device_id_type=MESH,
        )

    def seg_copy(d):
        src = segrow_ref if d == 1 else seg_buf.at[d - 2]
        return pltpu.make_async_remote_copy(
            src_ref=src, dst_ref=seg_buf.at[d - 1],
            send_sem=seg_ssem.at[d - 1], recv_sem=seg_rsem.at[d - 1],
            device_id={"inner": pos + 1}, device_id_type=MESH,
        )

    def sends(d):
        return (pos + 1 < n_in) & (pos >= d - 1)

    def back_receives(d):
        return (pos + 1 < n_in) & (pos + 1 >= d)

    def start_own(g):
        @pl.when(sends(1))
        def _():
            for c in range(2):
                kv_copy(g, c, 1).start()

    def forward(g):
        for d in range(1, reach):
            for c in range(2):
                @pl.when(pos >= d)
                def _():
                    kv_copy(g, c, d).wait_recv()

                @pl.when(sends(d + 1))
                def _():
                    kv_copy(g, c, d + 1).start()

    def farthest(g):
        @pl.when(pos >= reach)
        def _():
            for c in range(2):
                kv_copy(g, c, reach).wait_recv()

    start_own(0)

    @pl.when(sends(1))
    def _():
        seg_copy(1).start()

    for d in range(1, reach + 1):
        @pl.when(pos < d)
        def _():
            seg_buf[d - 1] = jnp.full(seg_buf.shape[1:], -1, jnp.int32)
            for g in range(kvl):
                kv_buf[g, d - 1] = jnp.zeros(kv_buf.shape[2:], kv_buf.dtype)

        @pl.when(jnp.logical_not(back_receives(d)))
        def _():
            for g in range(kvl):
                back_recv[g, d - 1] = jnp.zeros(back_recv.shape[2:], back_recv.dtype)

    for d in range(1, reach + 1):
        @pl.when(pos >= d)
        def _():
            seg_copy(d).wait_recv()

        if d < reach:
            @pl.when(sends(d + 1))
            def _():
                seg_copy(d + 1).start()
    forward(0)
    seg_col = jnp.transpose(jnp.broadcast_to(segrow_ref[0:1, :], (half, tok)))
    for j in range(gh):
        segq_ref[pl.ds(j, tok, stride=gh), :] = seg_col
    for load, buf, ref in zip(loads, (q_in, do_in), (q_ref, do_ref)):
        load.wait()
        for g in range(kvl):
            if native:
                wide = buf[:, g * gh:(g + 1) * gh, :].astype(jnp.float32)
                ref[g] = wide.reshape(tok * gh, head_dim).astype(ref.dtype)
            else:
                ref[g] = buf[g]
    if kvl > 1:
        @pl.when(sends(reach))
        def _():
            for c in range(2):
                kv_copy(0, c, reach).wait_send()

        for g in range(1, kvl):
            start_own(g)
    farthest(0)

    def block(g, c, d, rows):
        if d == 0:
            return kv_ref[g, c, rows, :]
        return kv_buf[g, d - 1, c, rows, :]

    low, high = slice(0, half), slice(half, tok)
    mixes = (low, high)

    for hf in range(2):
        rest = high if hf == 0 else low
        far = reach if hf == 0 else 0
        seg0 = segrow_ref[:, mixes[hf]]
        segr = seg_buf[reach - 1, :, mixes[hf]]
        segcat[hf, :, 0:half] = seg0
        segcat[hf, :, half:tok] = segr
        segcat[hf, :, tok:tok + half] = segrow_ref[:, rest] if far == 0 else seg_buf[reach - 1, :, rest]
        for d in range(1, reach):
            at = tok + half + (d - 1) * tok
            segcat[hf, :, at:at + tok] = seg_buf[d - 1]

    rows_half = half * gh
    rows = min(512, rows_half)
    chunks = rows_half // rows
    tokens = rows // gh

    def compute(g, hf):
        rest = high if hf == 0 else low
        far = reach if hf == 0 else 0
        for c, cat in ((0, kcat), (1, vcat)):
            cat[0:half, :] = block(g, c, 0, mixes[hf])
            cat[half:tok, :] = block(g, c, reach, mixes[hf])
            cat[tok:tok + half, :] = block(g, c, far, rest)
            for d in range(1, reach):
                at = tok + half + (d - 1) * tok
                cat[at:at + tok, :] = block(g, c, d, slice(None))

        def chunk(i, carry):
            local = pl.ds(pl.multiple_of(i * rows, rows), rows)
            where = pl.ds(pl.multiple_of(hf * rows_half + i * rows, rows), rows)
            q = q_ref[g, where, :]
            do = do_ref[g, where, :]
            row_tok = lax.broadcasted_iota(jnp.int32, (rows, half), 0) // gh + i * tokens
            causal = lax.broadcasted_iota(jnp.int32, (rows, half), 1) <= row_tok
            seg_q = segq_ref[where, :]

            def merge(full):
                return [jnp.where(causal, full[:, 0:half], full[:, half:tok])] + [
                    full[:, at:at + half] for at in range(tok, width + half, half)
                ]

            segs = [segcat[hf, 0:1, at:at + half] for at in range(0, width + half, half)]
            seg_k = [jnp.where(causal, segs[0], segs[1])] + segs[2:]
            scores = merge(dot(q, kcat[...], 1, 1))
            scores = [jnp.where(k == seg_q, s, MASKED) for k, s in zip(seg_k, scores)]
            top = jnp.max(functools.reduce(jnp.maximum, scores), 1, keepdims=True)
            es = [jnp.exp2((s - top) * (scale * math.log2(math.e))) for s in scores]
            total = jnp.sum(functools.reduce(jnp.add, es), 1, keepdims=True)
            inv = 1.0 / total
            ps = [e * inv for e in es]

            def spread(parts):
                own = jnp.where(causal, parts[0], 0.0)
                other = jnp.where(causal, 0.0, parts[0])
                return jnp.concatenate(
                    [x.astype(jnp.bfloat16) for x in [own, other] + parts[1:]], 1
                )

            pb = spread(ps)
            p_buf[local, :] = pb
            ob = dot(pb, vcat[...], 1, 0).astype(jnp.bfloat16)
            out_ref[g, where, :] = ob
            delta = jnp.sum(do.astype(jnp.float32) * ob.astype(jnp.float32), 1, keepdims=True)
            dps = merge(dot(do, vcat[...], 1, 1))
            dsb = spread([(p * scale) * (dp - delta) for p, dp in zip(ps, dps)])
            ds_buf[local, :] = dsb
            dq_ref[g, where, :] = dot(dsb, kcat[...], 1, 0).astype(jnp.bfloat16)
            return carry

        lax.fori_loop(0, chunks, chunk, 0)

    def weigh(g, hf, c):
        where = pl.ds(hf * rows_half, rows_half)
        if c == 0:
            dkcat[g, hf] = dot(ds_buf[...], q_ref[g, where, :], 0, 0)
        else:
            dvcat[g, hf] = dot(p_buf[...], do_ref[g, where, :], 0, 0)

    def partial(g, c, d, part):
        cat = (dkcat if c == 0 else dvcat).at[g]
        if d == 0:
            if part == 0:
                return cat[0, 0:half, :] + cat[1, tok:tok + half, :]
            return cat[1, 0:half, :]
        if d == reach:
            if part == 0:
                return cat[0, half:tok, :]
            return cat[1, half:tok, :] + cat[0, tok:tok + half, :]
        at = tok + half + (d - 1) * tok + part * half
        return cat[0, at:at + half, :] + cat[1, at:at + half, :]

    def back_copy(g, d, c, part):
        at = (g, d - 1, c, mixes[part])
        return pltpu.make_async_remote_copy(
            src_ref=back_send.at[at], dst_ref=back_recv.at[at],
            send_sem=b_ssem.at[g, d - 1, c, part], recv_sem=b_rsem.at[g, d - 1, c, part],
            device_id={"inner": pos - 1}, device_id_type=MESH,
        )

    def summed(g, d, c, part):
        term = partial(g, c, d, part)
        if d < reach:
            term = term + back_recv[g, d, c, mixes[part], :].astype(jnp.float32)
        return term

    def outer_copy(g, o, c, part):
        at = gather.at[slot + g, c, mixes[part]]
        return pltpu.make_async_remote_copy(
            src_ref=at, dst_ref=at,
            send_sem=g_ssem.at[g, o - 1, c, part], recv_sem=g_rsem.at[g, o - 1, c, part],
            device_id={"outer": lax.rem(outer + o, n_out)}, device_id_type=MESH,
        )

    def sibling_copy(g, o, c, part):
        src_outer = lax.rem(outer - o + n_out, n_out)
        at = gather.at[(src_outer * 2 + core) * kvl // share + g, c, mixes[part]]
        return pltpu.make_async_remote_copy(
            src_ref=at, dst_ref=at,
            send_sem=h_ssem.at[g, o, c, part], recv_sem=h_rsem.at[g, o, c, part],
            device_id={"heads": 1 - core}, device_id_type=MESH,
        )

    def share_copy(g, c, part):
        return pltpu.make_async_remote_copy(
            src_ref=gather.at[slot + g, c, mixes[part]], dst_ref=share_recv.at[g, c, mixes[part]],
            send_sem=h_ssem.at[g, 0, c, part], recv_sem=h_rsem.at[g, 0, c, part],
            device_id={"heads": 1 - core}, device_id_type=MESH,
        )

    pieces = [(c, part) for part in (0, 1) for c in (1, 0)]

    def step(g, d, c, part):
        if d < reach:
            @pl.when(back_receives(d + 1))
            def _():
                back_copy(g, d + 1, c, part).wait_recv()
        if d > 0:
            back_send[g, d - 1, c, mixes[part], :] = summed(g, d, c, part).astype(back_send.dtype)

            @pl.when(pos >= d)
            def _():
                back_copy(g, d, c, part).start()
            return
        own = gather.at[slot + g, c, mixes[part]]
        own[...] = summed(g, 0, c, part).astype(gather.dtype)
        if share > 1:
            copy = share_copy(g, c, part)
            copy.start()
            copy.wait()
            got = share_recv[g, c, mixes[part], :].astype(jnp.float32)
            own[...] = (own[...].astype(jnp.float32) + got).astype(gather.dtype)
        for o in range(1, n_out):
            outer_copy(g, o, c, part).start()
        if share == 1:
            sibling_copy(g, 0, c, part).start()

    def arrive(g):
        for c, part in pieces:
            for o in range(1, n_out):
                outer_copy(g, o, c, part).wait_recv()
                if share == 1:
                    sibling_copy(g, o, c, part).start()

    early = reach > 1
    for g in range(kvl):
        if g > 0:
            farthest(g)
        compute(g, 0)
        for c in (1, 0):
            weigh(g, 0, c)
            step(g, reach, c, 0)
        if g + 1 < kvl:
            forward(g + 1)
        if g > 0:
            for d in range(reach - 1, 0, -1):
                for c, part in pieces:
                    step(g - 1, d, c, part)
        compute(g, 1)
        for c in (1, 0):
            weigh(g, 1, c)
            step(g, reach, c, 1)
            if early and g + 1 == kvl:
                step(g, reach - 1, c, 0)
        if g > 0:
            for c, part in pieces:
                step(g - 1, 0, c, part)
    for buf, ref in ((out_ref, out_res), (dq_ref, dq_res)):
        if native:
            parts = [
                buf[g].astype(jnp.float32).reshape(tok, gh, head_dim) for g in range(kvl)
            ]
            ref[...] = jnp.concatenate(parts, 1).astype(ref.dtype)
        else:
            ref[...] = buf[...]
    for d in range(reach - 1, -1, -1):
        for c, part in pieces:
            if early and d == reach - 1 and part == 0:
                continue
            step(kvl - 1, d, c, part)
    for g in range(kvl):
        arrive(g)
    if share == 1:
        for g in range(kvl):
            for c, part in pieces:
                for o in range(n_out):
                    sibling_copy(g, o, c, part).wait_recv()
    kv_total = gather.shape[0]
    for c, ref in ((0, dk_res), (1, dv_res)):
        for k in range(kv_total):
            flat[c, pl.ds(k, tok, stride=kv_total), :] = gather[k, c].astype(jnp.float32)
        ref[...] = flat[c].reshape(ref.shape).astype(ref.dtype)

    for d in range(1, reach + 1):
        @pl.when(sends(d))
        def _():
            seg_copy(d).wait_send()
            for g in range(kvl):
                for c in range(2):
                    if kvl == 1 or g > 0 or d < reach:
                        kv_copy(g, c, d).wait_send()

        @pl.when(pos >= d)
        def _():
            for g in range(kvl):
                for c, part in pieces:
                    back_copy(g, d, c, part).wait_send()
    for g in range(kvl):
        for c, part in pieces:
            for o in range(1, n_out):
                outer_copy(g, o, c, part).wait_send()
            if share == 1:
                for o in range(n_out):
                    sibling_copy(g, o, c, part).wait_send()


def shards(queries, keys, values, grad_out, seg_ids):
    tok, heads, depth = queries.shape
    kv_total = keys.shape[1]
    gh = min(GROUP, heads)
    kvl = heads // gh
    share = GROUP // gh
    n_in, n_out = lax.axis_size("inner"), lax.axis_size("outer")
    reach = n_in // 2
    rows = tok * gh
    width = tok + (tok // 2) + tok * (reach - 1)
    wire = jnp.bfloat16 if reach <= 2 else jnp.float32

    def grouped(x):
        return x.reshape(tok, kvl, gh, depth).transpose(1, 0, 2, 3).reshape(kvl, rows, depth)

    def ungrouped(x):
        return x.reshape(kvl, tok, gh, depth).transpose(1, 0, 2, 3).reshape(tok, heads, depth)

    bf, f32 = jnp.bfloat16, jnp.float32
    dma = pltpu.SemaphoreType.DMA
    vmem = pl.BlockSpec(memory_space=pltpu.VMEM)
    acts = (tok, heads, depth) if gh % 8 == 0 else (kvl, rows, depth)
    held = pltpu.VMEM((kvl, rows, depth), bf)
    if gh % 8:
        queries, grad_out = grouped(queries), grouped(grad_out)
    out, dq, dk, dv = pl.pallas_call(
        functools.partial(kernel, (n_in, reach, n_out, kvl, gh, share, tok)),
        out_shape=tuple(
            jax.ShapeDtypeStruct(shape, bf) for shape in (acts, acts, keys.shape, keys.shape)
        ),
        in_specs=[pl.BlockSpec(memory_space=pl.ANY)] * 2 + [vmem] * 3,
        out_specs=(vmem,) * 4,
        scratch_shapes=[
            pltpu.VMEM(acts, bf), pltpu.VMEM(acts, bf), held, held, held, held,
            pltpu.VMEM((8, tok), jnp.int32), dma((2,)),
            pltpu.VMEM((kvl, 2, tok, depth), bf),
            pltpu.VMEM((rows, tok // 2), jnp.int32),
            pltpu.VMEM((2, tok * kv_total, depth), f32),
            pltpu.VMEM((kvl, reach, 2, tok, depth), bf),
            pltpu.VMEM((reach, 8, tok), jnp.int32),
            pltpu.VMEM((width, depth), bf),
            pltpu.VMEM((width, depth), bf),
            pltpu.VMEM((2, 8, width), jnp.int32),
            pltpu.VMEM((rows // 2, width), bf),
            pltpu.VMEM((rows // 2, width), bf),
            pltpu.VMEM((kvl, 2, width, depth), f32),
            pltpu.VMEM((kvl, 2, width, depth), f32),
            pltpu.VMEM((kvl, reach, 2, tok, depth), wire),
            pltpu.VMEM((kvl, reach, 2, tok, depth), wire),
            pltpu.VMEM((kv_total, 2, tok, depth), bf),
            pltpu.VMEM((kvl, 2, tok, depth), bf),
            dma((kvl, reach, 2)), dma((kvl, reach, 2)),
            dma((reach,)), dma((reach,)),
            dma((kvl, reach, 2, 2)), dma((kvl, reach, 2, 2)),
            dma((kvl, n_out, 2, 2)), dma((kvl, n_out, 2, 2)),
            dma((kvl, n_out, 2, 2)), dma((kvl, n_out, 2, 2)),
        ],
        compiler_params=pltpu.CompilerParams(
            collective_id=0, has_side_effects=True, vmem_limit_bytes=48 * 2**20
        ),
    )(queries, grad_out, keys, values, seg_ids[None, :])
    if gh % 8:
        out, dq = ungrouped(out), ungrouped(dq)
    return out, dq, dk, dv


def solution(mesh):
    act = P(("groups", "inner"), ("outer", "heads"), None)
    kv = P(("groups", "inner"), None, None)
    return jax.shard_map(
        shards,
        mesh=mesh,
        in_specs=(act, kv, kv, act, P(("groups", "inner"))),
        out_specs=(act, act, kv, kv),
        check_vma=False,
    )
```

```python
import functools
import math

import jax
import jax.numpy as jnp
from jax import lax
from jax.experimental import pallas as pl
from jax.experimental.pallas import tpu as pltpu
from jax.sharding import PartitionSpec as P

GROUP = 8
MASKED = -1e30
MESH = pl.DeviceIdType.MESH


def dot(a, b, ca, cb):
    return lax.dot_general(
        a, b, (((ca,), (cb,)), ((), ())), preferred_element_type=jnp.float32
    )


def kernel(
    cfg, q_arg, do_arg, key_ref, value_ref, seg_arg,
    out_res, dq_res, dk_res, dv_res,
    q_in, do_in, q_ref, do_ref, out_ref, dq_ref, segrow_ref, in_sem, kv_ref, segq_ref, flat, kv_buf, seg_buf, kcat, vcat, segcat, p_buf, ds_buf, dkcat, dvcat,
    back_send, back_recv, gather, share_recv,
    kv_ssem, kv_rsem, seg_ssem, seg_rsem, b_ssem, b_rsem, g_ssem, g_rsem, h_ssem, h_rsem,
):
    n_in, reach, n_out, kvl, gh, share, tok = cfg
    head_dim = q_ref.shape[-1]
    half = tok // 2
    native = gh % 8 == 0
    scale = head_dim ** (-0.5)
    width = half + half + tok * (reach - 1)
    pos = lax.axis_index("inner")
    outer = lax.axis_index("outer")
    core = lax.axis_index("heads")
    slot = (outer * 2 + core) * kvl // share

    loads = [
        pltpu.make_async_copy(arg, buf, in_sem.at[i])
        for i, (arg, buf) in enumerate(((q_arg, q_in), (do_arg, do_in)))
    ]
    for load in loads:
        load.start()
    segrow_ref[...] = jnp.broadcast_to(seg_arg[...], segrow_ref.shape)
    for c, ref in ((0, key_ref), (1, value_ref)):
        flat[c] = ref[...].astype(jnp.float32).reshape(flat.shape[1:])
        for g in range(kvl):
            kv_ref[g, c] = flat[c, pl.ds(slot + g, tok, stride=ref.shape[1]), :].astype(kv_ref.dtype)

    barrier = pltpu.get_barrier_semaphore()

    @pl.when(pos > 0)
    def _():
        pl.semaphore_signal(barrier, inc=1, device_id={"inner": pos - 1}, device_id_type=MESH)

    @pl.when(pos < n_in - 1)
    def _():
        pl.semaphore_signal(barrier, inc=1, device_id={"inner": pos + 1}, device_id_type=MESH)

    pl.semaphore_signal(barrier, inc=1, device_id={"heads": 1 - core}, device_id_type=MESH)
    for o in range(1, n_out):
        pl.semaphore_signal(
            barrier, inc=1, device_id={"outer": lax.rem(outer + o, n_out)}, device_id_type=MESH
        )
    ends = jnp.where(pos > 0, 1, 0) + jnp.where(pos < n_in - 1, 1, 0)
    pl.semaphore_wait(barrier, ends + n_out)

    def kv_copy(g, c, d):
        src = kv_ref.at[g, c] if d == 1 else kv_buf.at[g, d - 2, c]
        return pltpu.make_async_remote_copy(
            src_ref=src, dst_ref=kv_buf.at[g, d - 1, c],
            send_sem=kv_ssem.at[g, d - 1, c], recv_sem=kv_rsem.at[g, d - 1, c],
            device_id={"inner": pos + 1}, device_id_type=MESH,
        )

    def seg_copy(d):
        src = segrow_ref if d == 1 else seg_buf.at[d - 2]
        return pltpu.make_async_remote_copy(
            src_ref=src, dst_ref=seg_buf.at[d - 1],
            send_sem=seg_ssem.at[d - 1], recv_sem=seg_rsem.at[d - 1],
            device_id={"inner": pos + 1}, device_id_type=MESH,
        )

    def sends(d):
        return (pos + 1 < n_in) & (pos >= d - 1)

    def back_receives(d):
        return (pos + 1 < n_in) & (pos + 1 >= d)

    def start_own(g):
        @pl.when(sends(1))
        def _():
            for c in range(2):
                kv_copy(g, c, 1).start()

    def forward(g):
        for d in range(1, reach):
            for c in range(2):
                @pl.when(pos >= d)
                def _():
                    kv_copy(g, c, d).wait_recv()

                @pl.when(sends(d + 1))
                def _():
                    kv_copy(g, c, d + 1).start()

    def farthest(g):
        @pl.when(pos >= reach)
        def _():
            for c in range(2):
                kv_copy(g, c, reach).wait_recv()

    start_own(0)

    @pl.when(sends(1))
    def _():
        seg_copy(1).start()

    for d in range(1, reach + 1):
        @pl.when(pos < d)
        def _():
            seg_buf[d - 1] = jnp.full(seg_buf.shape[1:], -1, jnp.int32)
            for g in range(kvl):
                kv_buf[g, d - 1] = jnp.zeros(kv_buf.shape[2:], kv_buf.dtype)

        @pl.when(jnp.logical_not(back_receives(d)))
        def _():
            for g in range(kvl):
                back_recv[g, d - 1] = jnp.zeros(back_recv.shape[2:], back_recv.dtype)

    for d in range(1, reach + 1):
        @pl.when(pos >= d)
        def _():
            seg_copy(d).wait_recv()

        if d < reach:
            @pl.when(sends(d + 1))
            def _():
                seg_copy(d + 1).start()
    forward(0)
    seg_col = jnp.transpose(jnp.broadcast_to(segrow_ref[0:1, :], (half, tok)))
    for j in range(gh):
        segq_ref[pl.ds(j, tok, stride=gh), :] = seg_col
    for load, buf, ref in zip(loads, (q_in, do_in), (q_ref, do_ref)):
        load.wait()
        for g in range(kvl):
            if native:
                wide = buf[:, g * gh:(g + 1) * gh, :].astype(jnp.float32)
                ref[g] = wide.reshape(tok * gh, head_dim).astype(ref.dtype)
            else:
                ref[g] = buf[g]
    if kvl > 1:
        @pl.when(sends(reach))
        def _():
            for c in range(2):
                kv_copy(0, c, reach).wait_send()

        for g in range(1, kvl):
            start_own(g)
    farthest(0)

    def block(g, c, d, rows):
        if d == 0:
            return kv_ref[g, c, rows, :]
        return kv_buf[g, d - 1, c, rows, :]

    low, high = slice(0, half), slice(half, tok)
    mixes = (low, high)

    for hf in range(2):
        rest = high if hf == 0 else low
        far = reach if hf == 0 else 0
        seg0 = segrow_ref[:, mixes[hf]]
        segr = seg_buf[reach - 1, :, mixes[hf]]
        segcat[hf, :, 0:half] = seg0
        segcat[hf, :, half:tok] = segr
        segcat[hf, :, tok:tok + half] = segrow_ref[:, rest] if far == 0 else seg_buf[reach - 1, :, rest]
        for d in range(1, reach):
            at = tok + half + (d - 1) * tok
            segcat[hf, :, at:at + tok] = seg_buf[d - 1]

    rows_half = half * gh
    rows = rows_half
    chunks = rows_half // rows
    tokens = rows // gh

    def compute(g, hf):
        rest = high if hf == 0 else low
        far = reach if hf == 0 else 0
        for c, cat in ((0, kcat), (1, vcat)):
            cat[0:half, :] = block(g, c, 0, mixes[hf])
            cat[half:tok, :] = block(g, c, reach, mixes[hf])
            cat[tok:tok + half, :] = block(g, c, far, rest)
            for d in range(1, reach):
                at = tok + half + (d - 1) * tok
                cat[at:at + tok, :] = block(g, c, d, slice(None))

        def chunk(i, carry):
            local = pl.ds(pl.multiple_of(i * rows, rows), rows)
            where = pl.ds(pl.multiple_of(hf * rows_half + i * rows, rows), rows)
            q = q_ref[g, where, :]
            do = do_ref[g, where, :]
            row_tok = lax.broadcasted_iota(jnp.int32, (rows, half), 0) // gh + i * tokens
            causal = lax.broadcasted_iota(jnp.int32, (rows, half), 1) <= row_tok
            seg_q = segq_ref[where, :]

            def merge(full):
                return [jnp.where(causal, full[:, 0:half], full[:, half:tok])] + [
                    full[:, at:at + half] for at in range(tok, width + half, half)
                ]

            segs = [segcat[hf, 0:1, at:at + half] for at in range(0, width + half, half)]
            seg_k = [jnp.where(causal, segs[0], segs[1])] + segs[2:]
            scores = merge(dot(q, kcat[...], 1, 1))
            scores = [jnp.where(k == seg_q, s, MASKED) for k, s in zip(seg_k, scores)]
            top = jnp.max(functools.reduce(jnp.maximum, scores), 1, keepdims=True)
            es = [jnp.exp2((s - top) * (scale * math.log2(math.e))) for s in scores]
            total = jnp.sum(functools.reduce(jnp.add, es), 1, keepdims=True)
            inv = 1.0 / total
            ps = [e * inv for e in es]

            def spread(parts):
                own = jnp.where(causal, parts[0], 0.0)
                other = jnp.where(causal, 0.0, parts[0])
                return jnp.concatenate(
                    [x.astype(jnp.bfloat16) for x in [own, other] + parts[1:]], 1
                )

            pb = spread(ps)
            p_buf[local, :] = pb
            ob = dot(pb, vcat[...], 1, 0).astype(jnp.bfloat16)
            out_ref[g, where, :] = ob
            delta = jnp.sum(do.astype(jnp.float32) * ob.astype(jnp.float32), 1, keepdims=True)
            dps = merge(dot(do, vcat[...], 1, 1))
            dsb = spread([(p * scale) * (dp - delta) for p, dp in zip(ps, dps)])
            ds_buf[local, :] = dsb
            dq_ref[g, where, :] = dot(dsb, kcat[...], 1, 0).astype(jnp.bfloat16)
            return carry

        lax.fori_loop(0, chunks, chunk, 0)

    def weigh(g, hf, c):
        where = pl.ds(hf * rows_half, rows_half)
        if c == 0:
            dkcat[g, hf] = dot(ds_buf[...], q_ref[g, where, :], 0, 0)
        else:
            dvcat[g, hf] = dot(p_buf[...], do_ref[g, where, :], 0, 0)

    def partial(g, c, d, part):
        cat = (dkcat if c == 0 else dvcat).at[g]
        if d == 0:
            if part == 0:
                return cat[0, 0:half, :] + cat[1, tok:tok + half, :]
            return cat[1, 0:half, :]
        if d == reach:
            if part == 0:
                return cat[0, half:tok, :]
            return cat[1, half:tok, :] + cat[0, tok:tok + half, :]
        at = tok + half + (d - 1) * tok + part * half
        return cat[0, at:at + half, :] + cat[1, at:at + half, :]

    def back_copy(g, d, c, part):
        at = (g, d - 1, c, mixes[part])
        return pltpu.make_async_remote_copy(
            src_ref=back_send.at[at], dst_ref=back_recv.at[at],
            send_sem=b_ssem.at[g, d - 1, c, part], recv_sem=b_rsem.at[g, d - 1, c, part],
            device_id={"inner": pos - 1}, device_id_type=MESH,
        )

    def summed(g, d, c, part):
        term = partial(g, c, d, part)
        if d < reach:
            term = term + back_recv[g, d, c, mixes[part], :].astype(jnp.float32)
        return term

    def outer_copy(g, o, c, part):
        at = gather.at[slot + g, c, mixes[part]]
        return pltpu.make_async_remote_copy(
            src_ref=at, dst_ref=at,
            send_sem=g_ssem.at[g, o - 1, c, part], recv_sem=g_rsem.at[g, o - 1, c, part],
            device_id={"outer": lax.rem(outer + o, n_out)}, device_id_type=MESH,
        )

    def sibling_copy(g, o, c, part):
        src_outer = lax.rem(outer - o + n_out, n_out)
        at = gather.at[(src_outer * 2 + core) * kvl // share + g, c, mixes[part]]
        return pltpu.make_async_remote_copy(
            src_ref=at, dst_ref=at,
            send_sem=h_ssem.at[g, o, c, part], recv_sem=h_rsem.at[g, o, c, part],
            device_id={"heads": 1 - core}, device_id_type=MESH,
        )

    def share_copy(g, c, part):
        return pltpu.make_async_remote_copy(
            src_ref=gather.at[slot + g, c, mixes[part]], dst_ref=share_recv.at[g, c, mixes[part]],
            send_sem=h_ssem.at[g, 0, c, part], recv_sem=h_rsem.at[g, 0, c, part],
            device_id={"heads": 1 - core}, device_id_type=MESH,
        )

    pieces = [(c, part) for part in (0, 1) for c in (1, 0)]

    def step(g, d, c, part):
        if d < reach:
            @pl.when(back_receives(d + 1))
            def _():
                back_copy(g, d + 1, c, part).wait_recv()
        if d > 0:
            back_send[g, d - 1, c, mixes[part], :] = summed(g, d, c, part).astype(back_send.dtype)

            @pl.when(pos >= d)
            def _():
                back_copy(g, d, c, part).start()
            return
        own = gather.at[slot + g, c, mixes[part]]
        own[...] = summed(g, 0, c, part).astype(gather.dtype)
        if share > 1:
            copy = share_copy(g, c, part)
            copy.start()
            copy.wait()
            got = share_recv[g, c, mixes[part], :].astype(jnp.float32)
            own[...] = (own[...].astype(jnp.float32) + got).astype(gather.dtype)
        for o in range(1, n_out):
            outer_copy(g, o, c, part).start()
        if share == 1:
            sibling_copy(g, 0, c, part).start()

    def arrive(g):
        for c, part in pieces:
            for o in range(1, n_out):
                outer_copy(g, o, c, part).wait_recv()
                if share == 1:
                    sibling_copy(g, o, c, part).start()

    early = reach > 1
    for g in range(kvl):
        if g > 0:
            farthest(g)
        compute(g, 0)
        for c in (1, 0):
            weigh(g, 0, c)
            step(g, reach, c, 0)
        if g + 1 < kvl:
            forward(g + 1)
        if g > 0:
            for d in range(reach - 1, 0, -1):
                for c, part in pieces:
                    step(g - 1, d, c, part)
        compute(g, 1)
        for c in (1, 0):
            weigh(g, 1, c)
            step(g, reach, c, 1)
            if early and g + 1 == kvl:
                step(g, reach - 1, c, 0)
        if g > 0:
            for c, part in pieces:
                step(g - 1, 0, c, part)
    for buf, ref in ((out_ref, out_res), (dq_ref, dq_res)):
        if native:
            parts = [
                buf[g].astype(jnp.float32).reshape(tok, gh, head_dim) for g in range(kvl)
            ]
            ref[...] = jnp.concatenate(parts, 1).astype(ref.dtype)
        else:
            ref[...] = buf[...]
    for d in range(reach - 1, -1, -1):
        for c, part in pieces:
            if early and d == reach - 1 and part == 0:
                continue
            step(kvl - 1, d, c, part)
    for g in range(kvl):
        arrive(g)
    if share == 1:
        for g in range(kvl):
            for c, part in pieces:
                for o in range(n_out):
                    sibling_copy(g, o, c, part).wait_recv()
    kv_total = gather.shape[0]
    for c, ref in ((0, dk_res), (1, dv_res)):
        for k in range(kv_total):
            flat[c, pl.ds(k, tok, stride=kv_total), :] = gather[k, c].astype(jnp.float32)
        ref[...] = flat[c].reshape(ref.shape).astype(ref.dtype)

    for d in range(1, reach + 1):
        @pl.when(sends(d))
        def _():
            seg_copy(d).wait_send()
            for g in range(kvl):
                for c in range(2):
                    if kvl == 1 or g > 0 or d < reach:
                        kv_copy(g, c, d).wait_send()

        @pl.when(pos >= d)
        def _():
            for g in range(kvl):
                for c, part in pieces:
                    back_copy(g, d, c, part).wait_send()
    for g in range(kvl):
        for c, part in pieces:
            for o in range(1, n_out):
                outer_copy(g, o, c, part).wait_send()
            if share == 1:
                for o in range(n_out):
                    sibling_copy(g, o, c, part).wait_send()


def shards(queries, keys, values, grad_out, seg_ids):
    tok, heads, depth = queries.shape
    kv_total = keys.shape[1]
    gh = min(GROUP, heads)
    kvl = heads // gh
    share = GROUP // gh
    n_in, n_out = lax.axis_size("inner"), lax.axis_size("outer")
    reach = n_in // 2
    rows = tok * gh
    width = tok + (tok // 2) + tok * (reach - 1)
    wire = jnp.bfloat16 if reach <= 2 else jnp.float32

    def grouped(x):
        return x.reshape(tok, kvl, gh, depth).transpose(1, 0, 2, 3).reshape(kvl, rows, depth)

    def ungrouped(x):
        return x.reshape(kvl, tok, gh, depth).transpose(1, 0, 2, 3).reshape(tok, heads, depth)

    bf, f32 = jnp.bfloat16, jnp.float32
    dma = pltpu.SemaphoreType.DMA
    vmem = pl.BlockSpec(memory_space=pltpu.VMEM)
    acts = (tok, heads, depth) if gh % 8 == 0 else (kvl, rows, depth)
    held = pltpu.VMEM((kvl, rows, depth), bf)
    if gh % 8:
        queries, grad_out = grouped(queries), grouped(grad_out)
    out, dq, dk, dv = pl.pallas_call(
        functools.partial(kernel, (n_in, reach, n_out, kvl, gh, share, tok)),
        out_shape=tuple(
            jax.ShapeDtypeStruct(shape, bf) for shape in (acts, acts, keys.shape, keys.shape)
        ),
        in_specs=[pl.BlockSpec(memory_space=pl.ANY)] * 2 + [vmem] * 3,
        out_specs=(vmem,) * 4,
        scratch_shapes=[
            pltpu.VMEM(acts, bf), pltpu.VMEM(acts, bf), held, held, held, held,
            pltpu.VMEM((8, tok), jnp.int32), dma((2,)),
            pltpu.VMEM((kvl, 2, tok, depth), bf),
            pltpu.VMEM((rows, tok // 2), jnp.int32),
            pltpu.VMEM((2, tok * kv_total, depth), f32),
            pltpu.VMEM((kvl, reach, 2, tok, depth), bf),
            pltpu.VMEM((reach, 8, tok), jnp.int32),
            pltpu.VMEM((width, depth), bf),
            pltpu.VMEM((width, depth), bf),
            pltpu.VMEM((2, 8, width), jnp.int32),
            pltpu.VMEM((rows // 2, width), bf),
            pltpu.VMEM((rows // 2, width), bf),
            pltpu.VMEM((kvl, 2, width, depth), f32),
            pltpu.VMEM((kvl, 2, width, depth), f32),
            pltpu.VMEM((kvl, reach, 2, tok, depth), wire),
            pltpu.VMEM((kvl, reach, 2, tok, depth), wire),
            pltpu.VMEM((kv_total, 2, tok, depth), bf),
            pltpu.VMEM((kvl, 2, tok, depth), bf),
            dma((kvl, reach, 2)), dma((kvl, reach, 2)),
            dma((reach,)), dma((reach,)),
            dma((kvl, reach, 2, 2)), dma((kvl, reach, 2, 2)),
            dma((kvl, n_out, 2, 2)), dma((kvl, n_out, 2, 2)),
            dma((kvl, n_out, 2, 2)), dma((kvl, n_out, 2, 2)),
        ],
        compiler_params=pltpu.CompilerParams(
            collective_id=0, has_side_effects=True, vmem_limit_bytes=48 * 2**20
        ),
    )(queries, grad_out, keys, values, seg_ids[None, :])
    if gh % 8:
        out, dq = ungrouped(out), ungrouped(dq)
    return out, dq, dk, dv


def solution(mesh):
    act = P(("groups", "inner"), ("outer", "heads"), None)
    kv = P(("groups", "inner"), None, None)
    return jax.shard_map(
        shards,
        mesh=mesh,
        in_specs=(act, kv, kv, act, P(("groups", "inner"))),
        out_specs=(act, act, kv, kv),
        check_vma=False,
    )
```
